32 devices in a mesh: section: 2 (over core), head: 4 (over z), blk: 4 (over y, x).
Axes of the slice: x: 2, y: 2, z: 4, core: 2. Of those that a mesh axis runs over, the one named last changes fastest.
Arguments:
- section_input: bfloat16 [2, 8, 256, 1536], P('section', 'blk')
- modulation: bfloat16 [2, 8, 2, 1536], P('section', 'blk'), may hold values from -3 to 3
- attn_gate: bfloat16 [2, 8, 1536], P('section', 'blk'), may hold values from -12 to 12
- qkv_weight: bfloat16 [2, 1536, 3, 1536], P('section', None, None, 'head'), may hold values from -0.15625 to 0.15625
- out_weight: bfloat16 [2, 1536, 1536], P('section', 'head'), may hold values from -0.15625 to 0.15625
- kv_cache: bfloat16 [2, 8, 256, 4, 2, 1536], P('section', None, 'blk', None, None, 'head'), may hold values from -9 to 9
- text_kv: bfloat16 [2, 8, 154, 2, 1536], P('section', 'blk', None, None, 'head')
- text_len: int32 [8], P('blk'), may hold values from 4 to 154, as said below
- patch_order: int32 [4, 4], replicated, may hold values from 0 to 3, each once within a row
- final_mod: bfloat16 [8, 2, 1536], P('blk'), may hold values from -3 to 3
- final_weight: bfloat16 [1536, 64], replicated, may hold values from -0.15625 to 0.15625
- latent: float32 [4, 128, 128], P('blk', 'section'), may hold values from -6 to 6
Outputs:
- section_output: bfloat16 [2, 8, 256, 1536], P('section', 'blk', None, 'head')
- cache_patch: bfloat16 [2, 8, 256, 2, 1536], P('section', None, 'blk', None, 'head')
- latent_next: float32 [4, 128, 128], P('blk', 'section')
The draws below stay inside these ranges and needn't reach their ends.
Inputs may be any that keep to these rules, and one draw needn't show every extreme that they name: `text_len`: sequence 0 uses all 154 text positions. `patch_order`: each row is a permutation of the 4 patches.
All inputs are finite; a program needn't handle non-finite values.
Results may differ from the reference program's by a relative error of at most 0.0092.
Values may be sent and summed in bfloat16 or wider, within the bound.
A program may use at most 128 MiB of HBM per device.

```python
import math
import jax
import jax.numpy as jnp
from jax import lax

D = 1536
HEADS = 24
HEAD_DIM = 64
OUT_CH = 64
TXT = 154
NPATCH = 4
PT = 256
HID = 1536
IMAGES = 4
SEQS = 8
LAT_ROWS = 128
N_HEAD = 4


def draw_section_input(key, part):
    row_key, col_key, base_key = jax.random.split(key, 3)
    row_scale = jnp.exp(jax.random.uniform(row_key, (2, SEQS, PT, 1), jnp.float32, math.log(0.3), math.log(3.0)))
    col_scale = jnp.exp(jax.random.uniform(col_key, (1, 1, 1, D), jnp.float32, math.log(0.3), math.log(3.0)))
    base = jnp.clip(jax.random.normal(base_key, (2, SEQS, PT, D), jnp.float32), -4.0, 4.0)
    return (base * row_scale * col_scale).astype(jnp.bfloat16)


def draw_text_kv(key, part):
    base_key = jax.random.fold_in(key, 0)
    shape = (2, SEQS, TXT, 2, HID)
    base = jax.random.normal(base_key, shape, jnp.float32) * 1.5
    return jnp.clip(base, -9.0, 9.0).astype(jnp.bfloat16)


def draw_text_len(key, part):
    lengths = jax.random.randint(key, (SEQS,), 4, TXT + 1, dtype=jnp.int32)
    return lengths.at[0].set(TXT)


def level_of(stream_key, dims, cuts, smallest, top_value):
    factor_of = 1.0
    for axis_at, shards_of in cuts:
        steps = jax.random.uniform(jax.random.fold_in(jax.random.fold_in(stream_key, 6), axis_at), (shards_of,), jnp.float32, smallest / len(cuts), top_value / len(cuts))
        factor_of = factor_of * jnp.repeat(jnp.exp(steps), dims[axis_at] // shards_of).reshape((-1,) + (1,) * (len(dims) - 1 - axis_at))
    return factor_of


def scatter_about(stream_key, dims, width, most, cuts=(), kind=jnp.bfloat16):
    array = jax.random.normal(stream_key, dims, jnp.float32) * width
    if len(cuts) > 0:
        array = level_of(stream_key, dims, cuts, -0.22, 0.18) * array
    return jnp.clip(array, min=-most, max=most).astype(kind)


def setup_inputs(seed: int = 0) -> dict:
    key_list = jax.random.split(jax.random.key(seed), 13)
    return {
        "section_input": draw_section_input(jax.random.fold_in(key_list[12], 71), 0),
        "modulation": scatter_about(key_list[1], (2, SEQS, 2, D), 0.5, 3.0, ((0, 2), (1, 4))),
        "attn_gate": scatter_about(key_list[2], (2, SEQS, D), 2.0, 12.0, ((0, 2), (1, 4))),
        "qkv_weight": scatter_about(key_list[3], (2, D, 3, HID), D ** -0.5, 0.15625, ((0, 2), (3, 4))),
        "out_weight": scatter_about(key_list[4], (2, HID, D), HID ** -0.5, 0.15625, ((0, 2), (1, 4))),
        "kv_cache": scatter_about(key_list[5], (2, SEQS, PT, NPATCH, 2, HID), 1.5, 9.0, ((0, 2), (2, 4), (5, 4))),
        "text_kv": draw_text_kv(jax.random.fold_in(key_list[12], 71), 0),
        "text_len": draw_text_len(jax.random.fold_in(key_list[12], 71), 0),
        "patch_order": jax.vmap(lambda own: jax.random.permutation(own, NPATCH))(jax.random.split(key_list[8], IMAGES)).reshape((IMAGES, NPATCH)).astype(jnp.int32),
        "final_mod": scatter_about(key_list[9], (SEQS, 2, D), 0.5, 3.0, ((0, 4),)),
        "final_weight": scatter_about(key_list[10], (D, OUT_CH), D ** -0.5, 0.15625),
        "latent": scatter_about(key_list[11], (IMAGES, LAT_ROWS, 128), 1.0, 6.0, ((0, 4), (1, 2)), jnp.float32),
    }


norm_eps = 1e-06
guidance = 4.0
euler_step = -0.25

def layer_norm(values):
    row_mean = lax.optimization_barrier(jnp.mean(values, axis=-1, keepdims=True))
    centered = values - row_mean
    row_var = lax.optimization_barrier(jnp.mean(centered * centered, axis=-1, keepdims=True))
    return centered / jnp.sqrt(row_var + norm_eps)

def attend_one(queries, keys_all, values_all, length):
    total_keys = keys_all.shape[0]
    query_heads = queries.reshape(PT, HEADS, HEAD_DIM).astype(jnp.float32)
    key_heads = keys_all.reshape(total_keys, HEADS, HEAD_DIM).astype(jnp.float32)
    value_heads = values_all.reshape(total_keys, HEADS, HEAD_DIM).astype(jnp.float32)
    scores = jnp.einsum('qhd,khd->hqk', query_heads, key_heads) * HEAD_DIM ** (-0.5)
    positions = jnp.arange(total_keys, dtype=jnp.int32)
    counted = (positions >= TXT) | (positions < length)
    scores = jnp.where(counted[None, None, :], scores, -1e+30)
    row_max = lax.optimization_barrier(jnp.max(scores, axis=-1, keepdims=True))
    weights = jnp.exp(scores - row_max)
    attn_probs = (weights / lax.optimization_barrier(jnp.sum(weights, axis=-1, keepdims=True))).astype(jnp.bfloat16)
    attended = jnp.einsum('hqk,khd->qhd', attn_probs.astype(jnp.float32), value_heads)
    return attended.reshape(PT, HID).astype(jnp.bfloat16)

def reference(section_input, modulation, attn_gate, qkv_weight, out_weight, kv_cache, text_kv, text_len, patch_order, final_mod, final_weight, latent):
    group_width = HID // N_HEAD
    layer_outputs = []
    fresh_layers = []
    for layer_id in range(2):
        hidden_in = section_input[layer_id].astype(jnp.float32)
        shift_scale = modulation[layer_id].astype(jnp.float32)
        normed = (layer_norm(hidden_in) * (1.0 + shift_scale[:, 1:2]) + shift_scale[:, 0:1]).astype(jnp.bfloat16)
        projected = jnp.dot(normed.reshape(SEQS * PT, D), qkv_weight[layer_id].reshape(D, 3 * HID), preferred_element_type=jnp.float32).astype(jnp.bfloat16)
        projected = projected.reshape(SEQS, PT, 3, HID)
        queries = projected[:, :, 0]
        key_new = projected[:, :, 1]
        value_new = projected[:, :, 2]
        seq_patch = jnp.repeat(patch_order[:, layer_id], 2)
        layer_cache = kv_cache[layer_id]
        is_now = (jnp.arange(NPATCH, dtype=jnp.int32)[None, :] == seq_patch[:, None])[:, None, :, None]
        image_keys = jnp.where(is_now, key_new[:, :, None, :], layer_cache[:, :, :, 0])
        image_values = jnp.where(is_now, value_new[:, :, None, :], layer_cache[:, :, :, 1])
        keys_all = jnp.concatenate([text_kv[layer_id][:, :, 0], image_keys.reshape(SEQS, PT * NPATCH, HID)], axis=1)
        values_all = jnp.concatenate([text_kv[layer_id][:, :, 1], image_values.reshape(SEQS, PT * NPATCH, HID)], axis=1)
        attended = lax.map(lambda items: attend_one(items[0], items[1], items[2], items[3]), (queries, keys_all, values_all, text_len))
        flat_rows = attended.reshape(SEQS * PT, HID)
        summed = jnp.zeros((SEQS * PT, D), jnp.float32)
        for group_id in range(N_HEAD):
            lower = group_id * group_width
            block_term = jnp.dot(flat_rows[:, lower:lower + group_width], out_weight[layer_id][lower:lower + group_width], preferred_element_type=jnp.float32)
            rounded = lax.optimization_barrier(block_term.astype(jnp.bfloat16))
            summed = summed + rounded.astype(jnp.float32)
        gate_wide = attn_gate[layer_id].astype(jnp.float32)[:, None, :]
        layer_out = (hidden_in + gate_wide * summed.reshape(SEQS, PT, D)).astype(jnp.bfloat16)
        layer_outputs.append(layer_out)
        fresh_layers.append(jnp.stack([key_new, value_new], axis=2))
    section_output = jnp.stack([layer_outputs[1], layer_outputs[0]])
    cache_patch = jnp.stack(fresh_layers)
    final_shift = final_mod.astype(jnp.float32)
    final_normed = (layer_norm(layer_outputs[1].astype(jnp.float32)) * (1.0 + final_shift[:, 1:2]) + final_shift[:, 0:1]).astype(jnp.bfloat16)
    velocity = jnp.dot(final_normed.reshape(SEQS * PT, D), final_weight, preferred_element_type=jnp.float32)
    velocity = velocity.reshape(IMAGES, 2, PT * OUT_CH)
    guided = velocity[:, 1] + guidance * (velocity[:, 0] - velocity[:, 1])
    latent_next = latent + euler_step * guided.reshape(IMAGES, LAT_ROWS, 128)
    return (section_output, cache_patch, latent_next)
```

```python
import functools
import jax
import jax.numpy as jnp
from jax import lax
from jax.experimental import pallas as pl
from jax.experimental.pallas import tpu as pltpu
from jax.sharding import PartitionSpec as P

HEAD_DIM = 64
LANES = 128
TEXT_PAD = 256
norm_eps = 1e-06
guidance = 4.0
euler_step = -0.25
F32 = jnp.float32
BF16 = jnp.bfloat16
NT = (((1,), (1,)), ((), ()))


def dot(a, b):
    return jnp.dot(a, b, preferred_element_type=F32)


def kernel(
    n_blk, n_head, piece, rows,
    x_ref, mod_ref, gate_ref, wqkv_ref, wout_ref, stale_ref, text_ref, bias_ref,
    fmod_ref, fw_ref, latent_ref,
    recv_ref, fresh_out_ref, latent_out_ref,
    kv, queries, fresh, attended, part_send, part_land, own_out, vel_own, vel_land, guided_ref,
    stale_send, stale_recv, own_sem, fresh_send, fresh_recv, fresh_own,
    part_ssem, part_rsem, sec_ssem, sec_rsem, vel_ssem, vel_rsem,
):
    sec = lax.axis_index("section")
    head = lax.axis_index("head")
    blk = lax.axis_index("blk")
    seqs, tokens, width = x_ref.shape
    group = wqkv_ref.shape[2]
    base = TEXT_PAD + tokens
    half = tokens // 2

    barrier = pltpu.get_barrier_semaphore()
    for d in range(1, n_blk):
        pl.semaphore_signal(barrier, inc=1, device_id={"blk": lax.rem(blk + d, n_blk)})
    for d in range(1, n_head):
        pl.semaphore_signal(barrier, inc=1, device_id={"head": lax.rem(head + d, n_head)})
    pl.semaphore_signal(barrier, inc=1, device_id={"section": 1 - sec})
    pl.semaphore_wait(barrier, n_blk - 1 + n_head - 1 + 1)

    def place(src):
        return pl.ds(pl.multiple_of(base + src * piece, 16), piece)

    stale_copies = []
    for s in range(seqs):
        for d in range(1, n_blk):
            dst = lax.rem(blk + d, n_blk)
            copy = pltpu.make_async_remote_copy(
                src_ref=stale_ref.at[dst * seqs + s],
                dst_ref=kv.at[s, :, place(blk), :],
                send_sem=stale_send.at[s, d - 1],
                recv_sem=stale_recv.at[s, d - 1],
                device_id={"blk": dst},
            )
            copy.start()
            stale_copies.append(copy)
    own_copies = []
    for s in range(seqs):
        copy = pltpu.make_async_copy(
            stale_ref.at[blk * seqs + s], kv.at[s, :, place(blk), :], own_sem.at[s]
        )
        copy.start()
        own_copies.append(copy)

    for s in range(seqs):
        x = x_ref[s].astype(F32)
        mean = jnp.mean(x, axis=-1, keepdims=True)
        centered = x - mean
        var = jnp.mean(centered * centered, axis=-1, keepdims=True)
        inv = 1.0 / jnp.sqrt(var + norm_eps)
        normed = (centered * inv * (1.0 + mod_ref[s, 1:2, :]) + mod_ref[s, 0:1, :]).astype(BF16)
        queries[s] = (dot(normed, wqkv_ref[0]).astype(BF16) * 0.125).astype(BF16)
        for j in range(2):
            new = dot(normed, wqkv_ref[j + 1]).astype(BF16)
            kv[s, j, 0:TEXT_PAD, :] = text_ref[s, j]
            kv[s, j, TEXT_PAD:base, :] = new
            fresh[s, j] = new.astype(fresh.dtype)

    def fresh_rows(dst):
        return pl.ds(pl.multiple_of(dst * rows, 8), rows)

    fresh_copies = []
    for d in range(1, n_blk):
        dst = lax.rem(blk + d, n_blk)
        copy = pltpu.make_async_remote_copy(
            src_ref=fresh.at[:, :, fresh_rows(dst), :],
            dst_ref=fresh_out_ref.at[pl.ds(blk * seqs, seqs)],
            send_sem=fresh_send.at[d - 1],
            recv_sem=fresh_recv.at[d - 1],
            device_id={"blk": dst},
        )
        copy.start()
        fresh_copies.append(copy)
    own_fresh = pltpu.make_async_copy(
        fresh.at[:, :, fresh_rows(blk), :], fresh_out_ref.at[pl.ds(blk * seqs, seqs)], fresh_own
    )
    own_fresh.start()

    shift_term, scale_terms = [], []
    for s in range(seqs):
        lhs = jnp.broadcast_to(fmod_ref[s, 0:1, :], (8, width)).astype(BF16)
        shift_term.append(
            lax.dot_general(lhs, fw_ref[s], NT, preferred_element_type=F32)[0:1]
        )
        terms = []
        for g in range(n_head):
            cut = slice(g * group, (g + 1) * group)
            wide = jnp.broadcast_to(1.0 + fmod_ref[s, 1:2, cut], (8, group))
            high = wide.astype(BF16)
            low = (wide - high.astype(F32)).astype(BF16)
            w = fw_ref[s, :, cut]
            terms.append(
                (
                    lax.dot_general(high, w, NT, preferred_element_type=F32)
                    + lax.dot_general(low, w, NT, preferred_element_type=F32)
                )[0:1]
            )
        scale_terms.append(terms)

    lane = lax.broadcasted_iota(jnp.int32, (1, LANES), 1)
    low_half = lane < HEAD_DIM
    share = pl.ds(pl.multiple_of(head * group, LANES), group)
    part_copies = []
    for s in range(seqs):
        own_copies[s].wait()
        for d in range(1, n_blk):
            stale_copies[s * (n_blk - 1) + d - 1].wait_recv()
        bias = bias_ref[s]
        for p in range(group // LANES):
            cut = slice(p * LANES, (p + 1) * LANES)
            q = queries[s, :, cut]
            k = kv[s, 0, :, cut]
            v = kv[s, 1, :, cut]
            outs = []
            for side in (low_half, jnp.logical_not(low_half)):
                q_side = q * side.astype(BF16)
                scores = lax.dot_general(q_side, k, NT, preferred_element_type=F32) + bias
                top = jnp.max(scores, axis=-1, keepdims=True)
                weights = jnp.exp(scores - top)
                total = jnp.sum(weights, axis=-1, keepdims=True)
                outs.append(dot(weights.astype(BF16), v) / total)
            attended[s, :, cut] = jnp.where(low_half, outs[0], outs[1]).astype(BF16)
        att = attended[s]
        for g in range(n_head):
            part_send[s, g] = dot(att, wout_ref[:, g * group : (g + 1) * group]).astype(BF16)
        for d in range(1, n_head):
            dst = lax.rem(head + d, n_head)
            copy = pltpu.make_async_remote_copy(
                src_ref=part_send.at[s, dst],
                dst_ref=part_land.at[s, d - 1],
                send_sem=part_ssem.at[s, d - 1],
                recv_sem=part_rsem.at[s, d - 1],
                device_id={"head": dst},
            )
            copy.start()
            part_copies.append(copy)

    sec_copies = []
    for s in range(seqs):
        total = part_send[s, head].astype(F32)
        for d in range(1, n_head):
            part_copies[s * (n_head - 1) + d - 1].wait_recv()
            total = total + part_land[s, d - 1].astype(F32)
        own_out[s] = (x_ref[s, :, share].astype(F32) + gate_ref[s, :, share] * total).astype(BF16)
        copy = pltpu.make_async_remote_copy(
            src_ref=own_out.at[s],
            dst_ref=recv_ref.at[s],
            send_sem=sec_ssem.at[s],
            recv_sem=sec_rsem.at[s],
            device_id={"section": 1 - sec},
        )
        copy.start()
        sec_copies.append(copy)

    wide_lane = lax.broadcasted_iota(jnp.int32, (half, LANES), 1)
    stats = jnp.zeros((half, LANES), F32)
    product = jnp.zeros((half, LANES), F32)
    first = sec == 0
    for s in range(seqs):
        sec_copies[s].wait_recv()
        x = jnp.where(
            first, recv_ref[s, 0:half].astype(F32), own_out[s, half:tokens].astype(F32)
        )
        mean = jnp.mean(x, axis=-1, keepdims=True)
        centered = x - mean
        squares = jnp.sum(centered * centered, axis=-1, keepdims=True)
        scaled = (centered * (1.0 + fmod_ref[s, 1:2, share])).astype(BF16)
        product = product + lax.dot_general(
            scaled, fw_ref[s, :, share], NT, preferred_element_type=F32
        )
        stats = jnp.where(wide_lane == 2 * s, mean, stats)
        stats = jnp.where(wide_lane == 2 * s + 1, squares, stats)
    vel_own[:, 0:LANES] = product
    vel_own[:, LANES : 2 * LANES] = stats
    vel_copies = []
    for d in range(1, n_head):
        copy = pltpu.make_async_remote_copy(
            src_ref=vel_own,
            dst_ref=vel_land.at[head],
            send_sem=vel_ssem.at[d - 1],
            recv_sem=vel_rsem.at[d - 1],
            device_id={"head": lax.rem(head + d, n_head)},
        )
        copy.start()
        vel_copies.append(copy)
    for copy in vel_copies:
        copy.wait_recv()
    vel_land[head] = vel_own[...]
    velocity = jnp.zeros((half, LANES), F32)
    summed = vel_land[0, :, 0:LANES]
    for g in range(1, n_head):
        summed = summed + vel_land[g, :, 0:LANES]
    for s in range(seqs):
        means = [vel_land[g, :, LANES + 2 * s : LANES + 2 * s + 1] for g in range(n_head)]
        mean = sum(means) / n_head
        var = sum(
            vel_land[g, :, LANES + 2 * s + 1 : LANES + 2 * s + 2]
            + group * (means[g] - mean) * (means[g] - mean)
            for g in range(n_head)
        ) / width
        inv = 1.0 / jnp.sqrt(var + norm_eps)
        mine = low_half if s == 0 else jnp.logical_not(low_half)
        corrected = jnp.where(mine, summed, 0.0)
        for g in range(n_head):
            corrected = corrected + (means[g] - mean) * scale_terms[s][g]
        velocity = velocity + corrected * inv + shift_term[s]
    weighted = velocity * jnp.where(low_half, guidance, 1.0 - guidance)
    guided_ref[...] = weighted + pltpu.roll(weighted, HEAD_DIM, 1)
    even = guided_ref[pl.ds(0, half // 2, 2), :]
    odd = guided_ref[pl.ds(1, half // 2, 2), :]
    latent_out_ref[...] = latent_ref[...] + euler_step * jnp.where(low_half, even, odd)

    own_fresh.wait()
    for copy in fresh_copies:
        copy.wait()
    for copy in stale_copies + part_copies + sec_copies + vel_copies:
        copy.wait_send()


def shards(
    n_blk, n_head,
    section_input, modulation, attn_gate, qkv_weight, out_weight, kv_cache, text_kv,
    text_len, patch_order, final_mod, final_weight, latent,
):
    section_index = lax.axis_index("section")
    own_order = lax.dynamic_index_in_dim(patch_order, section_index, 1, keepdims=False)
    seq_patch = jnp.repeat(own_order, 2)
    x = section_input[0]
    seqs, tokens, width = x.shape
    group = qkv_weight.shape[3]
    cache = kv_cache[0]
    all_seqs, rows, patches = cache.shape[:3]
    kept = (patches - 1) * rows
    piece = -(-kept // 16) * 16
    at = seq_patch[:, None, None, None, None]
    stale = jnp.stack(
        [
            jnp.where(j < at[:, :, 0], cache[:, :, j], cache[:, :, j + 1])
            for j in range(patches - 1)
        ],
        axis=1,
    )
    stale = stale.transpose(0, 3, 1, 2, 4).reshape(all_seqs, 2, kept, group)
    stale = jnp.pad(stale, ((0, 0), (0, 0), (0, piece - kept), (0, 0)))
    text_count = text_kv.shape[2]
    text = jnp.pad(
        text_kv[0].transpose(0, 2, 1, 3), ((0, 0), (0, 0), (0, TEXT_PAD - text_count), (0, 0))
    )
    base = TEXT_PAD + tokens
    keys = base + n_blk * piece
    position = jnp.arange(keys, dtype=jnp.int32)[None, :]
    counted = jnp.where(
        position < base,
        (position >= TEXT_PAD) | (position < text_len[:, None]),
        (position - base) % piece < kept,
    )
    bias = jnp.where(counted, 0.0, -1e30).astype(F32)[:, None, :]
    weight_t = final_weight.T
    out_ch = weight_t.shape[0]
    final_t = jnp.stack(
        [jnp.pad(weight_t, ((0, out_ch), (0, 0))), jnp.pad(weight_t, ((out_ch, 0), (0, 0)))]
    )
    fresh_type = BF16 if rows % 16 == 0 else F32
    half = tokens // 2
    vmem = pl.BlockSpec(memory_space=pltpu.VMEM)
    dma = pltpu.SemaphoreType.DMA
    received, fresh, latent_next = pl.pallas_call(
        functools.partial(kernel, n_blk, n_head, piece, rows),
        out_shape=(
            jax.ShapeDtypeStruct((seqs, tokens, group), BF16),
            jax.ShapeDtypeStruct((all_seqs, 2, rows, group), fresh_type),
            jax.ShapeDtypeStruct(latent.shape[1:], F32),
        ),
        in_specs=[vmem] * 5 + [pl.BlockSpec(memory_space=pl.ANY)] + [vmem] * 5,
        out_specs=(vmem, vmem, vmem),
        scratch_shapes=[
            pltpu.VMEM((seqs, 2, keys, group), BF16),
            pltpu.VMEM((seqs, tokens, group), BF16),
            pltpu.VMEM((seqs, 2, tokens, group), fresh_type),
            pltpu.VMEM((seqs, tokens, group), BF16),
            pltpu.VMEM((seqs, n_head, tokens, group), BF16),
            pltpu.VMEM((seqs, n_head - 1, tokens, group), BF16),
            pltpu.VMEM((seqs, tokens, group), BF16),
            pltpu.VMEM((half, 2 * LANES), F32),
            pltpu.VMEM((n_head, half, 2 * LANES), F32),
            pltpu.VMEM((half, LANES), F32),
            dma((seqs, n_blk - 1)),
            dma((seqs, n_blk - 1)),
            dma((seqs,)),
            dma((n_blk - 1,)),
            dma((n_blk - 1,)),
            dma(()),
            dma((seqs, n_head - 1)),
            dma((seqs, n_head - 1)),
            dma((seqs,)),
            dma((seqs,)),
            dma((n_head - 1,)),
            dma((n_head - 1,)),
        ],
        compiler_params=pltpu.CompilerParams(
            collective_id=0, has_side_effects=True, vmem_limit_bytes=56 * 1024 * 1024
        ),
    )(
        x,
        modulation[0].astype(F32),
        attn_gate[0].astype(F32)[:, None, :],
        qkv_weight[0].transpose(1, 0, 2),
        out_weight[0],
        stale,
        text,
        bias,
        final_mod.astype(F32),
        final_t,
        latent[0],
    )
    cache_patch = fresh.astype(BF16).transpose(0, 2, 1, 3)
    return (received[None], cache_patch[None], latent_next[None])


def solution(mesh):
    placed = (
        P("section", "blk", None, None),
        P("section", "blk", None, None),
        P("section", "blk", None),
        P("section", None, None, "head"),
        P("section", "head", None),
        P("section", None, "blk", None, None, "head"),
        P("section", "blk", None, None, "head"),
        P("blk"),
        P(),
        P("blk", None, None),
        P(),
        P("blk", "section", None),
    )
    return jax.shard_map(
        functools.partial(shards, mesh.shape["blk"], mesh.shape["head"]),
        mesh=mesh,
        in_specs=placed,
        out_specs=(
            P("section", "blk", None, "head"),
            P("section", None, "blk", None, "head"),
            P("blk", "section", None),
        ),
        check_vma=False,
    )
```

```python
import functools
import math
import jax
import jax.numpy as jnp
from jax import lax
from jax.experimental import pallas as pl
from jax.experimental.pallas import tpu as pltpu
from jax.sharding import PartitionSpec as P

HEAD_DIM = 64
QUERY_SCALE = HEAD_DIM ** (-0.5) * math.log2(math.e)
LANES = 128
TEXT_PAD = 256
norm_eps = 1e-06
guidance = 4.0
euler_step = -0.25
F32 = jnp.float32
BF16 = jnp.bfloat16
NT = (((1,), (1,)), ((), ()))


def dot(a, b):
    return jnp.dot(a, b, preferred_element_type=F32)


def kernel(
    n_blk, n_head, piece, rows, padded,
    x_ref, mod_ref, gate_ref, wqkv_ref, wout_ref, stale_ref, text_ref, bias_ref,
    fmod_ref, fw_ref, latent_ref,
    recv_ref, fresh_out_ref, latent_out_ref,
    kv, queries, fresh, attended, part_send, part_land, own_out, vel_own, vel_land, stat_own, stat_land, guided_ref, fw_pad,
    stale_send, stale_recv, own_sem, fresh_send, fresh_recv, fresh_own,
    part_ssem, part_rsem, sec_ssem, sec_rsem, vel_ssem, vel_rsem,
):
    sec = lax.axis_index("section")
    head = lax.axis_index("head")
    blk = lax.axis_index("blk")
    seqs, tokens, width = x_ref.shape
    group = wqkv_ref.shape[2]
    base = TEXT_PAD + tokens
    half = tokens // 2

    barrier = pltpu.get_barrier_semaphore()
    for d in range(1, n_blk):
        pl.semaphore_signal(barrier, inc=1, device_id={"blk": lax.rem(blk + d, n_blk)})
    for d in range(1, n_head):
        pl.semaphore_signal(barrier, inc=1, device_id={"head": lax.rem(head + d, n_head)})
    pl.semaphore_signal(barrier, inc=1, device_id={"section": 1 - sec})
    pl.semaphore_wait(barrier, n_blk - 1 + n_head - 1 + 1)

    def place(src):
        return pl.ds(pl.multiple_of(base + src * piece, 16), piece)

    stale_copies = []
    for s in range(seqs):
        for d in range(1, n_blk):
            dst = lax.rem(blk + d, n_blk)
            copy = pltpu.make_async_remote_copy(
                src_ref=stale_ref.at[dst * seqs + s],
                dst_ref=kv.at[s, :, place(blk), :],
                send_sem=stale_send.at[s, d - 1],
                recv_sem=stale_recv.at[s, d - 1],
                device_id={"blk": dst},
            )
            copy.start()
            stale_copies.append(copy)
    own_copies = []
    for s in range(seqs):
        copy = pltpu.make_async_copy(
            stale_ref.at[blk * seqs + s], kv.at[s, :, place(blk), :], own_sem.at[s]
        )
        copy.start()
        own_copies.append(copy)

    for s in range(seqs):
        x = x_ref[s].astype(F32)
        mean = jnp.mean(x, axis=-1, keepdims=True)
        centered = x - mean
        var = jnp.mean(centered * centered, axis=-1, keepdims=True)
        inv = 1.0 / jnp.sqrt(var + norm_eps)
        shift_scale = mod_ref[s].astype(F32)
        normed = (centered * inv * (1.0 + shift_scale[1:2]) + shift_scale[0:1]).astype(BF16)
        queries[s] = (dot(normed, wqkv_ref[0]) * QUERY_SCALE).astype(BF16)
        for j in range(2):
            new = dot(normed, wqkv_ref[j + 1]).astype(BF16)
            kv[s, j, 0:TEXT_PAD, :] = text_ref[s, j]
            kv[s, j, TEXT_PAD:base, :] = new
            fresh[s, j] = new.astype(fresh.dtype)

    def fresh_rows(dst):
        return pl.ds(pl.multiple_of(dst * rows, 8), rows)

    fresh_copies = []
    for d in range(1, n_blk):
        dst = lax.rem(blk + d, n_blk)
        copy = pltpu.make_async_remote_copy(
            src_ref=fresh.at[:, :, fresh_rows(dst), :],
            dst_ref=fresh_out_ref.at[pl.ds(blk * seqs, seqs)],
            send_sem=fresh_send.at[d - 1],
            recv_sem=fresh_recv.at[d - 1],
            device_id={"blk": dst},
        )
        copy.start()
        fresh_copies.append(copy)
    own_fresh = pltpu.make_async_copy(
        fresh.at[:, :, fresh_rows(blk), :], fresh_out_ref.at[pl.ds(blk * seqs, seqs)], fresh_own
    )
    own_fresh.start()

    shift_term, scale_terms = [], []
    zeros = jnp.zeros(fw_ref.shape, BF16)
    for s in range(seqs):
        fw_pad[s] = jnp.concatenate([fw_ref[...], zeros] if s == 0 else [zeros, fw_ref[...]], axis=0)
        final_wide = fmod_ref[s].astype(F32)
        lhs = jnp.broadcast_to(final_wide[0:1], (8, width)).astype(BF16)
        shift_term.append(
            lax.dot_general(lhs, fw_pad[s], NT, preferred_element_type=F32)[0:1]
        )
        terms = []
        for g in range(n_head):
            cut = slice(g * group, (g + 1) * group)
            wide = jnp.broadcast_to(1.0 + final_wide[1:2, cut], (8, group))
            high = wide.astype(BF16)
            low = (wide - high.astype(F32)).astype(BF16)
            w = fw_pad[s, :, cut]
            terms.append(
                (
                    lax.dot_general(high, w, NT, preferred_element_type=F32)
                    + lax.dot_general(low, w, NT, preferred_element_type=F32)
                )[0:1]
            )
        scale_terms.append(terms)

    lane = lax.broadcasted_iota(jnp.int32, (1, LANES), 1)
    low_half = lane < HEAD_DIM
    share = pl.ds(pl.multiple_of(head * group, LANES), group)
    part_copies = []
    ones = jnp.ones((base - TEXT_PAD + n_blk * piece, LANES), BF16)
    for s in range(seqs):
        own_copies[s].wait()
        for d in range(1, n_blk):
            stale_copies[s * (n_blk - 1) + d - 1].wait_recv()
        for c in range(2):
            chunk = slice(c * half, (c + 1) * half)
            for p in range(group // LANES):
                cut = slice(p * LANES, (p + 1) * LANES)
                q = queries[s, chunk, cut]
                pair = jnp.concatenate(
                    [q * low_half.astype(BF16), q * jnp.logical_not(low_half).astype(BF16)], axis=0
                )
                text_scores = (
                    lax.dot_general(pair, kv[s, 0, 0:TEXT_PAD, cut], NT, preferred_element_type=F32)
                    + bias_ref[s, :, 0:TEXT_PAD]
                )
                scores = lax.dot_general(
                    pair, kv[s, 0, TEXT_PAD:, cut], NT, preferred_element_type=F32
                )
                if padded:
                    scores = scores + bias_ref[s, :, TEXT_PAD:]
                top = jnp.maximum(
                    jnp.max(text_scores, axis=-1, keepdims=True),
                    jnp.max(scores, axis=-1, keepdims=True),
                )
                text_weights = jnp.exp2(text_scores - top).astype(BF16)
                weights = jnp.exp2(scores - top).astype(BF16)
                text_v = jnp.concatenate([kv[s, 1, 0:TEXT_PAD, cut], ones[0:TEXT_PAD]], axis=1)
                v = jnp.concatenate([kv[s, 1, TEXT_PAD:, cut], ones], axis=1)
                acc = dot(text_weights, text_v) + dot(weights, v)
                out = acc[:, 0:LANES] / acc[:, LANES : 2 * LANES]
                attended[s, chunk, cut] = jnp.where(low_half, out[0:half], out[half:tokens]).astype(
                    BF16
                )
            att = attended[s, chunk]
            for g in range(n_head):
                part_send[s, c, g] = dot(att, wout_ref[:, g * group : (g + 1) * group]).astype(BF16)
            for d in range(1, n_head):
                dst = lax.rem(head + d, n_head)
                copy = pltpu.make_async_remote_copy(
                    src_ref=part_send.at[s, c, dst],
                    dst_ref=part_land.at[s, c, d - 1],
                    send_sem=part_ssem.at[s, c, d - 1],
                    recv_sem=part_rsem.at[s, c, d - 1],
                    device_id={"head": dst},
                )
                copy.start()
                part_copies.append(copy)

    sec_copies = []
    for s in range(seqs):
        for c in range(2):
            chunk = slice(c * half, (c + 1) * half)
            total = part_send[s, c, head].astype(F32)
            for d in range(1, n_head):
                part_copies[(s * 2 + c) * (n_head - 1) + d - 1].wait_recv()
                total = total + part_land[s, c, d - 1].astype(F32)
            gate = gate_ref[:, share].astype(F32)[s : s + 1]
            own_out[s, chunk] = (x_ref[s, chunk, share].astype(F32) + gate * total).astype(BF16)
            copy = pltpu.make_async_remote_copy(
                src_ref=own_out.at[s, chunk],
                dst_ref=recv_ref.at[s, chunk],
                send_sem=sec_ssem.at[s, c],
                recv_sem=sec_rsem.at[s, c],
                device_id={"section": 1 - sec},
            )
            copy.start()
            sec_copies.append(copy)

    wide_lane = lax.broadcasted_iota(jnp.int32, (half, LANES), 1)
    stats = jnp.zeros((half, LANES), F32)
    product = jnp.zeros((half, LANES), F32)
    first = sec == 0
    for s in range(seqs):
        for c in range(2):
            sec_copies[s * 2 + c].wait_recv()
        x = jnp.where(
            first, recv_ref[s, 0:half].astype(F32), own_out[s, half:tokens].astype(F32)
        )
        mean = jnp.mean(x, axis=-1, keepdims=True)
        centered = x - mean
        squares = jnp.sum(centered * centered, axis=-1, keepdims=True)
        scaled = (centered * (1.0 + fmod_ref[s, :, share].astype(F32)[1:2])).astype(BF16)
        product = product + lax.dot_general(
            scaled, fw_pad[s, :, share], NT, preferred_element_type=F32
        )
        stats = jnp.where(wide_lane == 2 * s, mean, stats)
        stats = jnp.where(wide_lane == 2 * s + 1, squares, stats)
    vel_own[...] = product.astype(BF16)
    stat_own[...] = stats.T[0:8]
    vel_copies = []
    for d in range(1, n_head):
        for j, (src, land) in enumerate(((vel_own, vel_land), (stat_own, stat_land))):
            copy = pltpu.make_async_remote_copy(
                src_ref=src,
                dst_ref=land.at[head],
                send_sem=vel_ssem.at[j, d - 1],
                recv_sem=vel_rsem.at[j, d - 1],
                device_id={"head": lax.rem(head + d, n_head)},
            )
            copy.start()
            vel_copies.append(copy)
    vel_land[head] = vel_own[...]
    stat_land[head] = stat_own[...]
    for copy in vel_copies:
        copy.wait_recv()
    summed = vel_land[0].astype(F32)
    for g in range(1, n_head):
        summed = summed + vel_land[g].astype(F32)
    row = lax.broadcasted_iota(jnp.int32, (LANES, half), 0)
    packed = jnp.zeros((LANES, half), F32)
    for s in range(seqs):
        means = [stat_land[g, 2 * s : 2 * s + 1, :] for g in range(n_head)]
        mean = sum(means) / n_head
        var = sum(
            stat_land[g, 2 * s + 1 : 2 * s + 2, :] + group * (means[g] - mean) * (means[g] - mean)
            for g in range(n_head)
        ) / width
        first_row = s * (n_head + 1)
        packed = jnp.where(row == first_row, 1.0 / jnp.sqrt(var + norm_eps), packed)
        for g in range(n_head):
            packed = jnp.where(row == first_row + 1 + g, means[g] - mean, packed)
    columns = packed.T
    velocity = jnp.zeros((half, LANES), F32)
    for s in range(seqs):
        at = s * (n_head + 1)
        mine = low_half if s == 0 else jnp.logical_not(low_half)
        corrected = jnp.where(mine, summed, 0.0)
        for g in range(n_head):
            corrected = corrected + columns[:, at + 1 + g : at + 2 + g] * scale_terms[s][g]
        velocity = velocity + corrected * columns[:, at : at + 1] + shift_term[s]
    weighted = velocity * jnp.where(low_half, guidance, 1.0 - guidance)
    guided_ref[...] = weighted + pltpu.roll(weighted, HEAD_DIM, 1)
    even = guided_ref[pl.ds(0, half // 2, 2), :]
    odd = guided_ref[pl.ds(1, half // 2, 2), :]
    latent_out_ref[...] = latent_ref[...] + euler_step * jnp.where(low_half, even, odd)

    own_fresh.wait()
    for copy in fresh_copies:
        copy.wait()
    for copy in stale_copies + part_copies + sec_copies + vel_copies:
        copy.wait_send()


def shards(
    n_blk, n_head,
    section_input, modulation, attn_gate, qkv_weight, out_weight, kv_cache, text_kv,
    text_len, patch_order, final_mod, final_weight, latent,
):
    section_index = lax.axis_index("section")
    own_order = lax.dynamic_index_in_dim(patch_order, section_index, 1, keepdims=False)
    seq_patch = jnp.repeat(own_order, 2)
    x = section_input[0]
    seqs, tokens, width = x.shape
    group = qkv_weight.shape[3]
    cache = kv_cache[0]
    all_seqs, rows, patches = cache.shape[:3]
    kept = (patches - 1) * rows
    piece = -(-kept // 16) * 16
    at = seq_patch[:, None, None, None, None]
    stale = jnp.stack(
        [
            jnp.where(j < at[:, :, 0], cache[:, :, j], cache[:, :, j + 1])
            for j in range(patches - 1)
        ],
        axis=1,
    )
    stale = stale.transpose(0, 3, 1, 2, 4).reshape(all_seqs, 2, kept, group)
    stale = jnp.pad(stale, ((0, 0), (0, 0), (0, piece - kept), (0, 0)))
    text_count = text_kv.shape[2]
    text = jnp.pad(
        text_kv[0].transpose(0, 2, 1, 3), ((0, 0), (0, 0), (0, TEXT_PAD - text_count), (0, 0))
    )
    base = TEXT_PAD + tokens
    keys = base + n_blk * piece
    position = jnp.arange(keys, dtype=jnp.int32)[None, :]
    counted = jnp.where(
        position < base,
        (position >= TEXT_PAD) | (position < text_len[:, None]),
        (position - base) % piece < kept,
    )
    bias = jnp.where(counted, 0.0, -1e30).astype(F32)[:, None, :]
    fresh_type = BF16 if rows % 16 == 0 else F32
    half = tokens // 2
    vmem = pl.BlockSpec(memory_space=pltpu.VMEM)
    dma = pltpu.SemaphoreType.DMA
    received, fresh, latent_next = pl.pallas_call(
        functools.partial(kernel, n_blk, n_head, piece, rows, piece != kept),
        out_shape=(
            jax.ShapeDtypeStruct((seqs, tokens, group), BF16),
            jax.ShapeDtypeStruct((all_seqs, 2, rows, group), fresh_type),
            jax.ShapeDtypeStruct(latent.shape[1:], F32),
        ),
        in_specs=[vmem] * 5 + [pl.BlockSpec(memory_space=pl.ANY)] + [vmem] * 5,
        out_specs=(vmem, vmem, vmem),
        scratch_shapes=[
            pltpu.VMEM((seqs, 2, keys, group), BF16),
            pltpu.VMEM((seqs, tokens, group), BF16),
            pltpu.VMEM((seqs, 2, tokens, group), fresh_type),
            pltpu.VMEM((seqs, tokens, group), BF16),
            pltpu.VMEM((seqs, 2, n_head, half, group), BF16),
            pltpu.VMEM((seqs, 2, n_head - 1, half, group), BF16),
            pltpu.VMEM((seqs, tokens, group), BF16),
            pltpu.VMEM((half, LANES), BF16),
            pltpu.VMEM((n_head, half, LANES), BF16),
            pltpu.VMEM((8, half), F32),
            pltpu.VMEM((n_head, 8, half), F32),
            pltpu.VMEM((half, LANES), F32),
            pltpu.VMEM((seqs, LANES, width), BF16),
            dma((seqs, n_blk - 1)),
            dma((seqs, n_blk - 1)),
            dma((seqs,)),
            dma((n_blk - 1,)),
            dma((n_blk - 1,)),
            dma(()),
            dma((seqs, 2, n_head - 1)),
            dma((seqs, 2, n_head - 1)),
            dma((seqs, 2)),
            dma((seqs, 2)),
            dma((2, n_head - 1)),
            dma((2, n_head - 1)),
        ],
        compiler_params=pltpu.CompilerParams(
            collective_id=0, has_side_effects=True, vmem_limit_bytes=56 * 1024 * 1024
        ),
    )(
        x,
        modulation[0],
        attn_gate[0],
        qkv_weight[0].transpose(1, 0, 2),
        out_weight[0],
        stale,
        text,
        bias,
        final_mod,
        final_weight.T,
        latent[0],
    )
    cache_patch = fresh.astype(BF16).transpose(0, 2, 1, 3)
    return (received[None], cache_patch[None], latent_next[None])


def solution(mesh):
    placed = (
        P("section", "blk", None, None),
        P("section", "blk", None, None),
        P("section", "blk", None),
        P("section", None, None, "head"),
        P("section", "head", None),
        P("section", None, "blk", None, None, "head"),
        P("section", "blk", None, None, "head"),
        P("blk"),
        P(),
        P("blk", None, None),
        P(),
        P("blk", "section", None),
    )
    return jax.shard_map(
        functools.partial(shards, mesh.shape["blk"], mesh.shape["head"]),
        mesh=mesh,
        in_specs=placed,
        out_specs=(
            P("section", "blk", None, "head"),
            P("section", None, "blk", None, "head"),
            P("blk", "section", None),
        ),
        check_vma=False,
    )
```

```python
import functools
import math
import jax
import jax.numpy as jnp
from jax import lax
from jax.experimental import pallas as pl
from jax.experimental.pallas import tpu as pltpu
from jax.sharding import PartitionSpec as P

HEAD_DIM = 64
QUERY_SCALE = HEAD_DIM ** (-0.5) * math.log2(math.e)
LANES = 128
TEXT_PAD = 256
norm_eps = 1e-06
guidance = 4.0
euler_step = -0.25
F32 = jnp.float32
BF16 = jnp.bfloat16
NT = (((1,), (1,)), ((), ()))


def dot(a, b):
    return jnp.dot(a, b, preferred_element_type=F32)


def kernel(
    n_blk, n_head, piece, rows, padded,
    x_ref, mod_ref, gate_ref, wqkv_ref, wout_ref, stale_ref, text_ref, bias_ref,
    fmod_ref, fw_ref, latent_ref,
    recv_ref, fresh_out_ref, latent_out_ref,
    kv, queries, fresh, attended, part_send, part_land, own_out, vel_own, vel_land, stat_own, stat_land, guided_ref, fw_pad,
    stale_send, stale_recv, own_sem, fresh_send, fresh_recv, fresh_own,
    part_ssem, part_rsem, sec_ssem, sec_rsem, vel_ssem, vel_rsem,
):
    sec = lax.axis_index("section")
    head = lax.axis_index("head")
    blk = lax.axis_index("blk")
    seqs, tokens, width = x_ref.shape
    group = wqkv_ref.shape[2]
    base = TEXT_PAD + tokens
    half = tokens // 2

    barrier = pltpu.get_barrier_semaphore()
    for d in range(1, n_blk):
        pl.semaphore_signal(barrier, inc=1, device_id={"blk": lax.rem(blk + d, n_blk)})
    for d in range(1, n_head):
        pl.semaphore_signal(barrier, inc=1, device_id={"head": lax.rem(head + d, n_head)})
    pl.semaphore_signal(barrier, inc=1, device_id={"section": 1 - sec})
    pl.semaphore_wait(barrier, n_blk - 1 + n_head - 1 + 1)

    def place(src):
        return pl.ds(pl.multiple_of(base + src * piece, 16), piece)

    stale_copies = []
    for s in range(seqs):
        for d in range(1, n_blk):
            dst = lax.rem(blk + d, n_blk)
            copy = pltpu.make_async_remote_copy(
                src_ref=stale_ref.at[dst * seqs + s],
                dst_ref=kv.at[s, :, place(blk), :],
                send_sem=stale_send.at[s, d - 1],
                recv_sem=stale_recv.at[s, d - 1],
                device_id={"blk": dst},
            )
            if s == 0:
                copy.start()
            stale_copies.append(copy)
    own_copies = []
    for s in range(seqs):
        copy = pltpu.make_async_copy(
            stale_ref.at[blk * seqs + s], kv.at[s, :, place(blk), :], own_sem.at[s]
        )
        copy.start()
        own_copies.append(copy)

    for s in range(seqs):
        x = x_ref[s].astype(F32)
        mean = jnp.mean(x, axis=-1, keepdims=True)
        centered = x - mean
        var = jnp.mean(centered * centered, axis=-1, keepdims=True)
        inv = 1.0 / jnp.sqrt(var + norm_eps)
        shift_scale = mod_ref[s].astype(F32)
        normed = (centered * inv * (1.0 + shift_scale[1:2]) + shift_scale[0:1]).astype(BF16)
        queries[s] = (dot(normed, wqkv_ref[0]) * QUERY_SCALE).astype(BF16)
        for j in range(2):
            new = dot(normed, wqkv_ref[j + 1]).astype(BF16)
            kv[s, j, 0:TEXT_PAD, :] = text_ref[s, j]
            kv[s, j, TEXT_PAD:base, :] = new
            fresh[s, j] = new.astype(fresh.dtype)

    for copy in stale_copies[: n_blk - 1]:
        copy.wait_send()
    for copy in stale_copies[n_blk - 1 :]:
        copy.start()

    shift_term, scale_terms = [], []
    zeros = jnp.zeros(fw_ref.shape, BF16)
    for s in range(seqs):
        fw_pad[s] = jnp.concatenate([fw_ref[...], zeros] if s == 0 else [zeros, fw_ref[...]], axis=0)
        final_wide = fmod_ref[s].astype(F32)
        lhs = jnp.broadcast_to(final_wide[0:1], (8, width)).astype(BF16)
        shift_term.append(
            lax.dot_general(lhs, fw_pad[s], NT, preferred_element_type=F32)[0:1]
        )
        terms = []
        for g in range(n_head):
            cut = slice(g * group, (g + 1) * group)
            wide = jnp.broadcast_to(1.0 + final_wide[1:2, cut], (8, group))
            high = wide.astype(BF16)
            low = (wide - high.astype(F32)).astype(BF16)
            w = fw_pad[s, :, cut]
            terms.append(
                (
                    lax.dot_general(high, w, NT, preferred_element_type=F32)
                    + lax.dot_general(low, w, NT, preferred_element_type=F32)
                )[0:1]
            )
        scale_terms.append(terms)

    lane = lax.broadcasted_iota(jnp.int32, (1, LANES), 1)
    low_half = lane < HEAD_DIM
    share = pl.ds(pl.multiple_of(head * group, LANES), group)
    def fresh_rows(dst):
        return pl.ds(pl.multiple_of(dst * rows, 8), rows)

    fresh_copies = []
    part_copies = []
    ones = jnp.ones((base - TEXT_PAD + n_blk * piece, LANES), BF16)
    for s in range(seqs):
        own_copies[s].wait()
        for d in range(1, n_blk):
            stale_copies[s * (n_blk - 1) + d - 1].wait_recv()
        for c in range(2):
            chunk = slice(c * half, (c + 1) * half)
            for p in range(group // LANES):
                cut = slice(p * LANES, (p + 1) * LANES)
                q = queries[s, chunk, cut]
                pair = jnp.concatenate(
                    [q * low_half.astype(BF16), q * jnp.logical_not(low_half).astype(BF16)], axis=0
                )
                text_scores = (
                    lax.dot_general(pair, kv[s, 0, 0:TEXT_PAD, cut], NT, preferred_element_type=F32)
                    + bias_ref[s, :, 0:TEXT_PAD]
                )
                scores = lax.dot_general(
                    pair, kv[s, 0, TEXT_PAD:, cut], NT, preferred_element_type=F32
                )
                if padded:
                    scores = scores + bias_ref[s, :, TEXT_PAD:]
                top = jnp.maximum(
                    jnp.max(text_scores, axis=-1, keepdims=True),
                    jnp.max(scores, axis=-1, keepdims=True),
                )
                text_weights = jnp.exp2(text_scores - top).astype(BF16)
                weights = jnp.exp2(scores - top).astype(BF16)
                text_v = jnp.concatenate([kv[s, 1, 0:TEXT_PAD, cut], ones[0:TEXT_PAD]], axis=1)
                v = jnp.concatenate([kv[s, 1, TEXT_PAD:, cut], ones], axis=1)
                acc = dot(text_weights, text_v) + dot(weights, v)
                out = acc[:, 0:LANES] / acc[:, LANES : 2 * LANES]
                attended[s, chunk, cut] = jnp.where(low_half, out[0:half], out[half:tokens]).astype(
                    BF16
                )
            att = attended[s, chunk]
            for g in range(n_head):
                part_send[s, c, g] = dot(att, wout_ref[:, g * group : (g + 1) * group]).astype(BF16)
            for d in range(1, n_head):
                dst = lax.rem(head + d, n_head)
                copy = pltpu.make_async_remote_copy(
                    src_ref=part_send.at[s, c, dst],
                    dst_ref=part_land.at[s, c, d - 1],
                    send_sem=part_ssem.at[s, c, d - 1],
                    recv_sem=part_rsem.at[s, c, d - 1],
                    device_id={"head": dst},
                )
                copy.start()
                part_copies.append(copy)
        if s == 0:
            for d in range(1, n_blk):
                dst = lax.rem(blk + d, n_blk)
                copy = pltpu.make_async_remote_copy(
                    src_ref=fresh.at[:, :, fresh_rows(dst), :],
                    dst_ref=fresh_out_ref.at[pl.ds(blk * seqs, seqs)],
                    send_sem=fresh_send.at[d - 1],
                    recv_sem=fresh_recv.at[d - 1],
                    device_id={"blk": dst},
                )
                copy.start()
                fresh_copies.append(copy)
            own_fresh = pltpu.make_async_copy(
                fresh.at[:, :, fresh_rows(blk), :], fresh_out_ref.at[pl.ds(blk * seqs, seqs)], fresh_own
            )
            own_fresh.start()

    sec_copies = []
    for s in range(seqs):
        for c in range(2):
            chunk = slice(c * half, (c + 1) * half)
            total = part_send[s, c, head].astype(F32)
            for d in range(1, n_head):
                part_copies[(s * 2 + c) * (n_head - 1) + d - 1].wait_recv()
                total = total + part_land[s, c, d - 1].astype(F32)
            gate = gate_ref[:, share].astype(F32)[s : s + 1]
            own_out[s, chunk] = (x_ref[s, chunk, share].astype(F32) + gate * total).astype(BF16)
            copy = pltpu.make_async_remote_copy(
                src_ref=own_out.at[s, chunk],
                dst_ref=recv_ref.at[s, chunk],
                send_sem=sec_ssem.at[s, c],
                recv_sem=sec_rsem.at[s, c],
                device_id={"section": 1 - sec},
            )
            copy.start()
            sec_copies.append(copy)

    wide_lane = lax.broadcasted_iota(jnp.int32, (half, LANES), 1)
    stats = jnp.zeros((half, LANES), F32)
    product = jnp.zeros((half, LANES), F32)
    first = sec == 0
    for s in range(seqs):
        for c in range(2):
            sec_copies[s * 2 + c].wait_recv()
        x = jnp.where(
            first, recv_ref[s, 0:half].astype(F32), own_out[s, half:tokens].astype(F32)
        )
        mean = jnp.mean(x, axis=-1, keepdims=True)
        centered = x - mean
        squares = jnp.sum(centered * centered, axis=-1, keepdims=True)
        scaled = (centered * (1.0 + fmod_ref[s, :, share].astype(F32)[1:2])).astype(BF16)
        product = product + lax.dot_general(
            scaled, fw_pad[s, :, share], NT, preferred_element_type=F32
        )
        stats = jnp.where(wide_lane == 2 * s, mean, stats)
        stats = jnp.where(wide_lane == 2 * s + 1, squares, stats)
    vel_own[...] = product.astype(BF16)
    stat_own[...] = stats.T[0:8]
    vel_copies = []
    for d in range(1, n_head):
        for j, (src, land) in enumerate(((vel_own, vel_land), (stat_own, stat_land))):
            copy = pltpu.make_async_remote_copy(
                src_ref=src,
                dst_ref=land.at[head],
                send_sem=vel_ssem.at[j, d - 1],
                recv_sem=vel_rsem.at[j, d - 1],
                device_id={"head": lax.rem(head + d, n_head)},
            )
            copy.start()
            vel_copies.append(copy)
    vel_land[head] = vel_own[...]
    stat_land[head] = stat_own[...]
    for copy in vel_copies:
        copy.wait_recv()
    summed = vel_land[0].astype(F32)
    for g in range(1, n_head):
        summed = summed + vel_land[g].astype(F32)
    row = lax.broadcasted_iota(jnp.int32, (LANES, half), 0)
    packed = jnp.zeros((LANES, half), F32)
    for s in range(seqs):
        means = [stat_land[g, 2 * s : 2 * s + 1, :] for g in range(n_head)]
        mean = sum(means) / n_head
        var = sum(
            stat_land[g, 2 * s + 1 : 2 * s + 2, :] + group * (means[g] - mean) * (means[g] - mean)
            for g in range(n_head)
        ) / width
        first_row = s * (n_head + 1)
        packed = jnp.where(row == first_row, 1.0 / jnp.sqrt(var + norm_eps), packed)
        for g in range(n_head):
            packed = jnp.where(row == first_row + 1 + g, means[g] - mean, packed)
    columns = packed.T
    velocity = jnp.zeros((half, LANES), F32)
    for s in range(seqs):
        at = s * (n_head + 1)
        mine = low_half if s == 0 else jnp.logical_not(low_half)
        corrected = jnp.where(mine, summed, 0.0)
        for g in range(n_head):
            corrected = corrected + columns[:, at + 1 + g : at + 2 + g] * scale_terms[s][g]
        velocity = velocity + corrected * columns[:, at : at + 1] + shift_term[s]
    weighted = velocity * jnp.where(low_half, guidance, 1.0 - guidance)
    guided_ref[...] = weighted + pltpu.roll(weighted, HEAD_DIM, 1)
    even = guided_ref[pl.ds(0, half // 2, 2), :]
    odd = guided_ref[pl.ds(1, half // 2, 2), :]
    latent_out_ref[...] = latent_ref[...] + euler_step * jnp.where(low_half, even, odd)

    own_fresh.wait()
    for copy in fresh_copies:
        copy.wait()
    for copy in stale_copies[n_blk - 1 :] + part_copies + sec_copies + vel_copies:
        copy.wait_send()


def shards(
    n_blk, n_head,
    section_input, modulation, attn_gate, qkv_weight, out_weight, kv_cache, text_kv,
    text_len, patch_order, final_mod, final_weight, latent,
):
    section_index = lax.axis_index("section")
    own_order = lax.dynamic_index_in_dim(patch_order, section_index, 1, keepdims=False)
    seq_patch = jnp.repeat(own_order, 2)
    x = section_input[0]
    seqs, tokens, width = x.shape
    group = qkv_weight.shape[3]
    cache = kv_cache[0]
    all_seqs, rows, patches = cache.shape[:3]
    kept = (patches - 1) * rows
    piece = -(-kept // 16) * 16
    before = jnp.arange(patches - 1, dtype=jnp.int32)[None, :] < seq_patch[:, None]
    stale = jnp.where(before[:, None, :, None, None], cache[:, :, :-1], cache[:, :, 1:])
    stale = stale.transpose(0, 3, 1, 2, 4).reshape(all_seqs, 2, kept, group)
    stale = jnp.pad(stale, ((0, 0), (0, 0), (0, piece - kept), (0, 0)))
    text_count = text_kv.shape[2]
    text = jnp.pad(
        text_kv[0].transpose(0, 2, 1, 3), ((0, 0), (0, 0), (0, TEXT_PAD - text_count), (0, 0))
    )
    base = TEXT_PAD + tokens
    keys = base + n_blk * piece
    position = jnp.arange(keys, dtype=jnp.int32)[None, :]
    counted = jnp.where(
        position < base,
        (position >= TEXT_PAD) | (position < text_len[:, None]),
        (position - base) % piece < kept,
    )
    bias = jnp.where(counted, 0.0, -1e30).astype(F32)[:, None, :]
    fresh_type = BF16 if rows % 16 == 0 else F32
    half = tokens // 2
    vmem = pl.BlockSpec(memory_space=pltpu.VMEM)
    dma = pltpu.SemaphoreType.DMA
    received, fresh, latent_next = pl.pallas_call(
        functools.partial(kernel, n_blk, n_head, piece, rows, piece != kept),
        out_shape=(
            jax.ShapeDtypeStruct((seqs, tokens, group), BF16),
            jax.ShapeDtypeStruct((all_seqs, 2, rows, group), fresh_type),
            jax.ShapeDtypeStruct(latent.shape[1:], F32),
        ),
        in_specs=[vmem] * 5 + [pl.BlockSpec(memory_space=pl.ANY)] + [vmem] * 5,
        out_specs=(vmem, vmem, vmem),
        scratch_shapes=[
            pltpu.VMEM((seqs, 2, keys, group), BF16),
            pltpu.VMEM((seqs, tokens, group), BF16),
            pltpu.VMEM((seqs, 2, tokens, group), fresh_type),
            pltpu.VMEM((seqs, tokens, group), BF16),
            pltpu.VMEM((seqs, 2, n_head, half, group), BF16),
            pltpu.VMEM((seqs, 2, n_head - 1, half, group), BF16),
            pltpu.VMEM((seqs, tokens, group), BF16),
            pltpu.VMEM((half, LANES), BF16),
            pltpu.VMEM((n_head, half, LANES), BF16),
            pltpu.VMEM((8, half), F32),
            pltpu.VMEM((n_head, 8, half), F32),
            pltpu.VMEM((half, LANES), F32),
            pltpu.VMEM((seqs, LANES, width), BF16),
            dma((seqs, n_blk - 1)),
            dma((seqs, n_blk - 1)),
            dma((seqs,)),
            dma((n_blk - 1,)),
            dma((n_blk - 1,)),
            dma(()),
            dma((seqs, 2, n_head - 1)),
            dma((seqs, 2, n_head - 1)),
            dma((seqs, 2)),
            dma((seqs, 2)),
            dma((2, n_head - 1)),
            dma((2, n_head - 1)),
        ],
        compiler_params=pltpu.CompilerParams(
            collective_id=0, has_side_effects=True, vmem_limit_bytes=56 * 1024 * 1024
        ),
    )(
        x,
        modulation[0],
        attn_gate[0],
        qkv_weight[0].transpose(1, 0, 2),
        out_weight[0],
        stale,
        text,
        bias,
        final_mod,
        final_weight.T,
        latent[0],
    )
    cache_patch = fresh.astype(BF16).transpose(0, 2, 1, 3)
    return (received[None], cache_patch[None], latent_next[None])


def solution(mesh):
    placed = (
        P("section", "blk", None, None),
        P("section", "blk", None, None),
        P("section", "blk", None),
        P("section", None, None, "head"),
        P("section", "head", None),
        P("section", None, "blk", None, None, "head"),
        P("section", "blk", None, None, "head"),
        P("blk"),
        P(),
        P("blk", None, None),
        P(),
        P("blk", "section", None),
    )
    return jax.shard_map(
        functools.partial(shards, mesh.shape["blk"], mesh.shape["head"]),
        mesh=mesh,
        in_specs=placed,
        out_specs=(
            P("section", "blk", None, "head"),
            P("section", None, "blk", None, "head"),
            P("blk", "section", None),
        ),
        check_vma=False,
    )
```
